256 devices in a mesh: outer: 8 (over y, x_hi), dp: 16 (over z, core), tensor: 2 (over x_lo).
Axes of the slice: x: 4 (x_hi: 2, x_lo: 2; x = x_hi * 2 + x_lo), y: 4, z: 8, core: 2. Of those that a mesh axis runs over, the one named last changes fastest.
Arguments:
- attn_out: bfloat16 [16384, 8192], P(('outer', 'dp')), may hold values from -24 to 24
- cotangent: bfloat16 [16384, 4096], P(('outer', 'dp'), 'tensor'), may hold values from -10 to 10
- out_weight: bfloat16 [8192, 4096], P('dp', 'tensor'), may hold values from -0.09375 to 0.09375
Outputs:
- input_grad: bfloat16 [16384, 8192], P(('outer', 'dp'))
- weight_grad: bfloat16 [8192, 4096], P('dp', 'tensor')
The draws below stay inside these ranges and needn't reach their ends.
All inputs are finite; a program needn't handle non-finite values.
Results may differ from the reference program's by a relative error of at most 0.018.
Values may be sent and summed in bfloat16 or wider, within the bound.
A program may use at most 64 MiB of HBM per device.

```python
import math
import jax
import jax.numpy as jnp
from jax import lax

DW = 4096
BLOCK = 128
HD = 8192
TOKENS = 16384
N_OUTER = 8


def draw_cotangent(key, part):
    key = jax.random.fold_in(key, 11)
    scale_key, value_key = jax.random.split(key)
    spread = jax.random.uniform(scale_key, (DW,), jnp.float32)
    column_scale = 0.25 * jnp.exp(spread * math.log(10.0))
    values = jnp.clip(jax.random.normal(value_key, (TOKENS, DW), jnp.float32), -4.0, 4.0)
    return (values * column_scale[None, :]).astype(jnp.bfloat16)


def strengthened(values, key, source, target, blocks, factor):
    def block_of(dim):
        return (jnp.arange(values.shape[dim]) // (values.shape[dim] // blocks)).reshape((-1,) + (1,) * (values.ndim - 1 - dim))

    one_side = jax.random.permutation(key, blocks)[block_of(target)]
    far = (block_of(target) + blocks // 2) % blocks
    return jnp.where((block_of(source) == one_side) | (block_of(source) == far), factor * values, values)


def steps_of(rng, extent, shards, least, top_value):
    gain = 1.0
    for axis_at, shards_of in shards:
        steps = jax.random.uniform(jax.random.fold_in(jax.random.fold_in(rng, 6), axis_at), (shards_of,), jnp.float32, least / len(shards), top_value / len(shards))
        gain = gain * jnp.repeat(jnp.exp(steps), extent[axis_at] // shards_of).reshape((-1,) + (1,) * (len(extent) - 1 - axis_at))
    return gain


def noise(stream_key, extent, deviation, bound, shards=(), kind=jnp.bfloat16):
    array = deviation * jax.random.normal(stream_key, extent, jnp.float32)
    if shards:
        array = array * steps_of(stream_key, extent, shards, -0.22, 0.18)
    return jnp.clip(array, -bound, bound).astype(kind)


def heavy_noise(stream_key, shape, scale, most, cuts, heavy, kind=jnp.bfloat16):
    result = scale * jax.random.normal(stream_key, shape, jnp.float32)
    if cuts:
        result = result * steps_of(stream_key, shape, cuts, -0.22, 0.18)
    return jnp.clip(strengthened(result, jax.random.fold_in(stream_key, 3), *heavy), -most, most).astype(kind)


def setup_inputs(seed: int = 0) -> dict:
    key_list = jax.random.split(jax.random.key(seed), 4)
    attn_out = heavy_noise(key_list[0], (TOKENS, HD), 1.0, 24.0, ((0, 128),), (0, 1, 128, 5.5))
    cotangent = draw_cotangent(jax.random.fold_in(key_list[3], 71), 0)
    out_weight = noise(key_list[2], (HD, DW), DW ** -0.5, 0.09375, ((0, 16), (1, 2)))
    return dict(attn_out=attn_out, cotangent=cotangent, out_weight=out_weight)


clip_ratio = 2.5

def hadamard(length):
    numbers = jnp.arange(length, dtype=jnp.int32)
    common = jnp.bitwise_and(numbers[:, None], numbers[None, :])
    parity = jnp.zeros_like(common)
    for position in range(int(length).bit_length()):
        parity = parity + jnp.bitwise_and(jnp.right_shift(common, position), 1)
    signs_table = 1.0 - 2.0 * jnp.bitwise_and(parity, 1).astype(jnp.float32)
    return signs_table / math.sqrt(length)

def rotate(matrix, table):
    height = matrix.shape[0]
    blocks = matrix.reshape(height, -1, table.shape[0])
    turned = jnp.einsum('rbk,kj->rbj', blocks, table, precision=lax.Precision.HIGHEST)
    return turned.reshape(height, -1)

def clip_blocks(matrix, width):
    height = matrix.shape[0]
    blocks = matrix.reshape(height, -1, width)
    mean_square = lax.optimization_barrier(jnp.mean(blocks * blocks, axis=-1, keepdims=True))
    limit = clip_ratio * jnp.sqrt(mean_square + 1e-06)
    return jnp.clip(blocks, -limit, limit).reshape(height, -1)

def reference(attn_out, cotangent, out_weight):
    input_grad = jnp.dot(cotangent, out_weight.T, preferred_element_type=jnp.float32).astype(jnp.bfloat16)
    table = hadamard(BLOCK)
    factor = TOKENS ** (-0.5)
    pods_act = attn_out.reshape(N_OUTER, -1, HD)
    pods_cot = cotangent.reshape(N_OUTER, -1, DW)

    def one_pod(total, pieces):
        pod_grad = jnp.dot(pieces[0].T, pieces[1], preferred_element_type=jnp.float32) * factor
        turned = rotate(pod_grad, table)
        rotated = clip_blocks(turned, BLOCK).astype(jnp.bfloat16)
        rotated = lax.optimization_barrier(rotated)
        return (total + rotated.astype(jnp.float32), None)
    total, unused = lax.scan(one_pod, jnp.zeros((HD, DW), jnp.float32), (pods_act, pods_cot))
    weight_grad = rotate(total, table).astype(jnp.bfloat16)
    return (input_grad, weight_grad)
```

```python
import functools

import jax
import jax.numpy as jnp
from jax import lax
from jax.experimental import pallas as pl
from jax.experimental.pallas import tpu as pltpu
from jax.sharding import PartitionSpec as P

MESH = pl.DeviceIdType.MESH
F32, BF16 = jnp.float32, jnp.bfloat16
NZ = 8
BLOCK = 128
TOK = 128
DCOL = 2048
HROW = 512
HALF = 256
CLIP = 2.5


def signs():
    row = lax.broadcasted_iota(jnp.int32, (BLOCK, BLOCK), 0)
    col = lax.broadcasted_iota(jnp.int32, (BLOCK, BLOCK), 1)
    common = row & col
    common = common ^ (common >> 4)
    common = common ^ (common >> 2)
    common = common ^ (common >> 1)
    return (1 - 2 * (common & 1)).astype(F32).astype(BF16)


def dot(a, b):
    return jnp.dot(a, b, preferred_element_type=F32)


def kernel(attn, cot, w, out, outw, COT, WV, WRT, ACT, AT, PART, PSEND, PRECV, OSEND, WG, RS1, RS2, RSX, S2, SX, FIN,
           ring_s, ring_r, sib_s, sib_r, att_s, att_r, arl_s, arl_r, par_s, par_r, out_s, out_r, orl_s, orl_r,
           rs_s, rs_r, ag_s, ag_r, loc):
    outer, me, t = lax.axis_index("outer"), lax.axis_index("dp"), lax.axis_index("tensor")
    z, c = me // 2, me % 2
    y, xh = outer // 2, outer % 2
    sib = z * 2 + 1 - c
    b1 = (y % 2 + y // 2) % 2
    b2 = y // 2
    y1 = y + 1 - 2 * (y % 2)
    y3 = 3 - y
    factor = (TOK * 2 * NZ * 8) ** (-0.5)

    def remote(src, dst, ssem, rsem, where):
        return pltpu.make_async_remote_copy(
            src_ref=src, dst_ref=dst, send_sem=ssem, recv_sem=rsem, device_id=where, device_id_type=MESH)

    def zdev(k):
        return {"dp": k}

    peer = {"tensor": 1 - t}

    def zat(dz):
        return (z + dz + 2 * NZ) % NZ

    def rows(ref, at, count, unit=None):
        return ref.at[pl.ds(pl.multiple_of(at, unit or count), count), :]

    barrier = pltpu.get_barrier_semaphore()

    def greet(k, carry):
        pl.semaphore_signal(barrier, inc=1, device_id={"dp": (me + k) % (2 * NZ)}, device_id_type=MESH)
        return carry

    lax.fori_loop(1, 2 * NZ, greet, 0)
    pl.semaphore_signal(barrier, inc=1, device_id=peer, device_id_type=MESH)
    for where in (y1 * 2 + xh, y3 * 2 + xh, y * 2 + 1 - xh):
        pl.semaphore_signal(barrier, inc=1, device_id={"outer": where}, device_id_type=MESH)

    load_w = pltpu.make_async_copy(w, WV, loc.at[0])
    load_w.start()
    own_act = pltpu.make_async_copy(
        attn.at[:, pl.ds(pl.multiple_of(me * HROW, HROW), HROW)], rows(ACT, me * TOK, TOK), loc.at[1])
    own_act.start()

    S = signs()
    for b in range(DCOL // BLOCK):
        part = slice(b * BLOCK, (b + 1) * BLOCK)
        COT[pl.ds(pl.multiple_of(me * TOK, TOK), TOK), part] = (dot(cot[:, part], S) * 0.125).astype(BF16)

    pl.semaphore_wait(barrier, 2 * NZ - 1 + 4)

    def ring(direction, step, half):
        sgn = 1 - 2 * direction
        block = rows(COT, (zat(-sgn * step) * 2 + c) * TOK + half * 64, 64)
        at = direction * 8 + step * 2 + half
        return remote(block, block, ring_s.at[at], ring_r.at[at], zdev(zat(sgn) * 2 + c))

    def ring_in(direction, step, half):
        sgn = 1 - 2 * direction
        block = rows(COT, (zat(-sgn * (step + 1)) * 2 + c) * TOK + half * 64, 64)
        at = direction * 8 + step * 2 + half
        return remote(block, block, ring_s.at[at], ring_r.at[at], zdev(zat(sgn) * 2 + c))

    LAST = ((0, 0), (1, 1))

    def sib_copy(dz, core):
        at = dz % NZ
        block = rows(COT, (zat(dz) * 2 + core) * TOK, TOK)
        return remote(block, block, sib_s.at[at], sib_r.at[at], zdev(sib))

    def other(k, dz):
        return zat((1 - 2 * (k // 2)) * dz) * 2 + k % 2

    def count(dz):
        return 2 if dz == NZ // 2 else 4

    def att_copy(to):
        src = attn.at[pl.ds(pl.multiple_of(t * 64, 64), 64), pl.ds(pl.multiple_of(to * HROW, HROW), HROW)]
        return remote(src, rows(ACT, me * TOK + t * 64, 64), att_s.at[to], att_r.at[me], zdev(to))

    def att_in(j):
        block = rows(ACT, j * TOK + t * 64, 64)
        return remote(block, block, att_s.at[j], att_r.at[j], zdev(j))

    def arl_copy(j):
        block = rows(ACT, j * TOK + t * 64, 64)
        return remote(block, block, arl_s.at[j], arl_r.at[j], peer)

    def arl_in(j):
        block = rows(ACT, j * TOK + (1 - t) * 64, 64)
        return remote(block, block, arl_s.at[j], arl_r.at[j], peer)

    def sib_att():
        return remote(attn.at[:, pl.ds(pl.multiple_of(sib * HROW, HROW), HROW)], rows(ACT, me * TOK, TOK),
                      att_s.at[sib], att_r.at[me], zdev(sib))

    def sib_att_in():
        block = rows(ACT, sib * TOK, TOK)
        return remote(block, block, att_s.at[sib], att_r.at[sib], zdev(sib))

    def over(dz, body):
        def step(k, carry):
            body(other(k, dz))
            return carry
        lax.fori_loop(0, count(dz), step, 0)

    def att_send(dz):
        over(dz, lambda j: att_copy(j).start())

    def att_relay(dz):
        def body(j):
            att_in(j).wait_recv()
            arl_copy(j).start()
        over(dz, body)

    def turn(j):
        AT[:, pl.ds(pl.multiple_of(j * TOK, TOK), TOK)] = ACT[pl.ds(pl.multiple_of(j * TOK, TOK), TOK), :].T

    def att_finish(dz):
        def body(j):
            arl_in(j).wait_recv()
            turn(j)
        over(dz, body)

    def par_copy(zz):
        return remote(rows(PSEND, zz * HALF, HALF), rows(PRECV, zz * HALF, HALF), par_s.at[zz], par_r.at[zz], peer)

    def process(zz):
        at = pl.ds(pl.multiple_of(zz * HALF, HALF), HALF)
        x = COT[at, :]
        PSEND[at, :] = dot(x, WRT[:, pl.ds(pl.multiple_of((1 - t) * HALF, HALF), HALF)]).astype(BF16)
        par_copy(zz).start()
        PART[at, :] = dot(x, WRT[:, pl.ds(pl.multiple_of(t * HALF, HALF), HALF)])

    def mine(j):
        return out.at[:, pl.ds(pl.multiple_of(j * HROW + t * HALF, HALF), HALF)]

    def theirs(j):
        return out.at[:, pl.ds(pl.multiple_of(j * HROW + (1 - t) * HALF, HALF), HALF)]

    def out_copy(to):
        return remote(rows(OSEND, to * TOK, TOK), mine(me), out_s.at[to], out_r.at[me], zdev(to))

    def out_in(j):
        return remote(mine(j), mine(j), out_s.at[j], out_r.at[j], zdev(j))

    def orl_copy(j, src=None):
        return remote(mine(j) if src is None else src, mine(j), orl_s.at[j], orl_r.at[j], peer)

    def orl_in(j):
        return remote(theirs(j), theirs(j), orl_s.at[j], orl_r.at[j], peer)

    own_out = pltpu.make_async_copy(rows(OSEND, me * TOK, TOK), mine(me), loc.at[2])

    def out_sum(zz):
        par_copy(zz).wait_recv()
        at = pl.ds(pl.multiple_of(zz * HALF, HALF), HALF)
        OSEND[at, :] = (PART[at, :] + PRECV[at, :].astype(F32)).astype(BF16)

    def out_stage(zz):
        out_sum(zz)
        out_copy(zz * 2).start()
        out_copy(zz * 2 + 1).start()

    def out_relay(dz):
        def body(j):
            out_in(j).wait_recv()
            orl_copy(j).start()
        over(dz, body)

    for half in range(2):
        for direction in range(2):
            ring(direction, 0, half).start()
    sib_copy(0, c).start()
    sib_att().start()
    att_send(4)

    load_w.wait()
    for b in range(DCOL // BLOCK):
        part = slice(b * BLOCK, (b + 1) * BLOCK)
        turned = lax.dot_general(S, WV[:, part], (((0,), (1,)), ((), ())), preferred_element_type=F32)
        WRT[part, :] = (turned * 0.0625).astype(BF16)
    sib_copy(0, 1 - c).wait_recv()
    process(z)
    own_act.wait()
    turn(me)

    for step in range(1, 4):
        for half in range(2):
            for direction in range(2):
                ring_in(direction, step - 1, half).wait_recv()
                if step < 3 or (direction, half) in LAST:
                    ring(direction, step, half).start()
        sib_copy(-step, c).start()
        sib_copy(step, c).start()
        att_send(4 - step)
        att_relay(5 - step)
        if step == 1:
            sib_att_in().wait_recv()
            turn(sib)
        else:
            att_finish(6 - step)
        sib_copy(-step, 1 - c).wait_recv()
        process(zat(-step))
        sib_copy(step, 1 - c).wait_recv()
        process(zat(step))

    for direction, half in LAST:
        ring_in(direction, 3, half).wait_recv()
    sib_copy(4, c).start()
    att_relay(1)
    out_sum(z)
    own_out.start()
    out_copy(sib).start()
    orl_copy(me, rows(OSEND, me * TOK, TOK)).start()
    att_finish(2)
    sib_copy(4, 1 - c).wait_recv()
    process(zat(4))
    for dz in (3, -3, 2, -2):
        out_stage(zat(dz))
    att_finish(1)

    ones = jnp.ones((BLOCK, BLOCK), BF16)
    scale = factor * 8.0 * BLOCK ** (-0.5)

    def weight(ch):
        def piece(n, carry):
            at = pl.multiple_of(n * 512, 512)
            acc = dot(AT[ch * HALF:(ch + 1) * HALF, :], COT[:, pl.ds(at, 512)]) * scale
            clipped = []
            for b in range(4):
                x = acc[:, b * BLOCK:(b + 1) * BLOCK]
                mean = dot((x * x).astype(BF16), ones) * (1.0 / BLOCK)
                limit = CLIP * jnp.sqrt(mean + 1e-6)
                clipped.append(jnp.clip(x, -limit, limit).astype(BF16))
            WG[ch * HALF:(ch + 1) * HALF, pl.ds(at, 512)] = jnp.concatenate(clipped, axis=1)
            return carry
        lax.fori_loop(0, DCOL // 512, piece, 0)

    def pick(half, a, b):
        return (1 - half) * a + half * b

    def place(i):
        half = i % 2
        p1, p2 = pick(half, y1, y3) * 2 + xh, pick(half, y3, y1) * 2 + xh
        return p1, p2, pick(half, b1, b2), pick(half, b2, b1), i * 128

    px = {"outer": y * 2 + 1 - xh}

    def ds16(at, n):
        return pl.ds(pl.multiple_of(at, 16), n)

    def rs1_copy(i):
        p1, p2, q1, q2, base = place(i)
        return remote(WG.at[ds16(base + (1 - q1) * 64, 64), :], RS1.at[ds16(i * 64, 64), :],
                      rs_s.at[i], rs_r.at[i], {"outer": p1})

    def rs2_copy(i):
        p1, p2, q1, q2, base = place(i)
        return remote(S2.at[ds16(i * 32, 32), :], RS2.at[ds16(i * 32, 32), :], rs_s.at[4 + i], rs_r.at[4 + i], {"outer": p2})

    def rsx_copy(i):
        return remote(SX.at[ds16(i * 16, 16), :], RSX.at[ds16(i * 16, 16), :], rs_s.at[8 + i], rs_r.at[8 + i], px)

    def combos(body):
        def step(i, carry):
            body(i)
            return carry
        lax.fori_loop(0, 4, step, 0)

    def stage2(i):
        p1, p2, q1, q2, base = place(i)
        rs1_copy(i).wait_recv()
        off = (1 - q2) * 32
        S2[ds16(i * 32, 32), :] = (WG[ds16(base + q1 * 64 + off, 32), :].astype(F32)
                                   + RS1[ds16(i * 64 + off, 32), :].astype(F32)).astype(BF16)
        rs2_copy(i).start()

    def three(i, row):
        p1, p2, q1, q2, base = place(i)
        return (WG[ds16(base + q1 * 64 + q2 * 32 + row, 16), :].astype(F32)
                + RS1[ds16(i * 64 + q2 * 32 + row, 16), :].astype(F32)
                + RS2[ds16(i * 32 + row, 16), :].astype(F32))

    def stage3(i):
        rs2_copy(i).wait_recv()
        SX[ds16(i * 16, 16), :] = three(i, (1 - xh) * 16).astype(BF16)
        rsx_copy(i).start()

    def ag_row(i, f1, f2, fx):
        p1, p2, q1, q2, base = place(i)
        a = q1 if f1 == 0 else 1 - q1
        b = q2 if f2 == 0 else 1 - q2
        d = xh if fx == 0 else 1 - xh
        return outw.at[ds16(base + a * 64 + b * 32 + d * 16, 16), :]

    KIND = ((0, 0, 0), (0, 0, 0), (0, 0, 0), (0, 0, 1), (0, 0, 1), (0, 1, 0), (0, 1, 1))
    FLIP = ((0, 0, 1), (0, 1, 0), (1, 0, 0), (0, 1, 1), (1, 0, 1), (1, 1, 0), (1, 1, 1))

    def ag_dev(i, kind):
        p1, p2, q1, q2, base = place(i)
        if kind == 0:
            return px
        return {"outer": p2 if kind in (1, 3) else p1}

    def ag_copy(i, kind, src=None):
        row = ag_row(i, *KIND[kind])
        return remote(row if src is None else src, row, ag_s.at[i * 7 + kind], ag_r.at[i * 7 + kind], ag_dev(i, kind))

    def ag_in(i, kind):
        row = ag_row(i, *FLIP[kind])
        return remote(row, row, ag_s.at[i * 7 + kind], ag_r.at[i * 7 + kind], ag_dev(i, kind))

    def own_fin(i):
        return pltpu.make_async_copy(FIN.at[ds16(i * 16, 16), :], ag_row(i, 0, 0, 0), loc.at[3 + i])

    def stage4(i):
        rsx_copy(i).wait_recv()
        total = three(i, xh * 16) + RSX[ds16(i * 16, 16), :].astype(F32)
        high = total.astype(BF16)
        low = (total - high.astype(F32)).astype(BF16)
        both = jnp.concatenate([high, low], axis=0)
        pieces = []
        for b in range(DCOL // BLOCK):
            r = dot(both[:, b * BLOCK:(b + 1) * BLOCK], S)
            pieces.append(((r[:16] + r[16:]) * (BLOCK ** (-0.5))).astype(BF16))
        FIN[ds16(i * 16, 16), :] = jnp.concatenate(pieces, axis=1)
        for kind in range(3):
            ag_copy(i, kind, FIN.at[ds16(i * 16, 16), :]).start()
        own_fin(i).start()

    def stage5(i):
        ag_in(i, 0).wait_recv()
        ag_copy(i, 3).start()
        ag_copy(i, 4).start()

    def stage6(i):
        ag_in(i, 1).wait_recv()
        ag_copy(i, 5).start()
        ag_in(i, 3).wait_recv()
        ag_copy(i, 6).start()

    def stage7(i):
        for kind in (2, 4, 5, 6):
            ag_in(i, kind).wait_recv()

    for ch in range(2):
        weight(ch)
        rs1_copy(ch * 2).start()
        rs1_copy(ch * 2 + 1).start()
    for dz in (4, 1, -1):
        out_stage(zat(dz))

    combos(stage2)
    out_in(sib).wait_recv()
    orl_copy(sib).start()
    out_relay(3)
    combos(stage3)
    out_relay(2)
    combos(stage4)
    out_relay(1)
    combos(stage5)
    combos(stage6)
    out_relay(4)
    combos(stage7)

    def all_j(body):
        def step(k, carry):
            body(k)
            return carry
        lax.fori_loop(0, 2 * NZ, step, 0)

    all_j(lambda j: orl_in(j).wait_recv())
    own_out.wait()
    for half in range(2):
        for direction in range(2):
            for step in range(4):
                if step < 3 or (direction, half) in LAST:
                    ring(direction, step, half).wait_send()
    for dz in range(NZ):
        sib_copy(dz, c).wait_send()
    sib_att().wait_send()
    out_copy(sib).wait_send()
    for dz in range(1, 5):
        def body(j):
            att_copy(j).wait_send()
            arl_copy(j).wait_send()
            out_copy(j).wait_send()
        over(dz, body)
    all_j(lambda j: orl_copy(j).wait_send())

    def parts(zz, carry):
        par_copy(zz).wait_send()
        return carry

    lax.fori_loop(0, NZ, parts, 0)

    def sums(i):
        rs1_copy(i).wait_send()
        rs2_copy(i).wait_send()
        rsx_copy(i).wait_send()
        for kind in range(7):
            ag_copy(i, kind).wait_send()
        own_fin(i).wait()

    combos(sums)


def local(attn_out, cotangent, out_weight):
    hbm, vmem = pl.BlockSpec(memory_space=pl.ANY), pl.BlockSpec(memory_space=pltpu.VMEM)
    dma = pltpu.SemaphoreType.DMA
    tokens = TOK * 2 * NZ
    return pl.pallas_call(
        kernel,
        out_shape=(jax.ShapeDtypeStruct(attn_out.shape, BF16), jax.ShapeDtypeStruct(out_weight.shape, BF16)),
        in_specs=[hbm, vmem, hbm],
        out_specs=(hbm, hbm),
        scratch_shapes=[
            pltpu.VMEM((tokens, DCOL), BF16),
            pltpu.VMEM((HROW, DCOL), BF16),
            pltpu.VMEM((DCOL, HROW), BF16),
            pltpu.VMEM((tokens, HROW), BF16),
            pltpu.VMEM((HROW, tokens), BF16),
            pltpu.VMEM((tokens, HALF), F32),
            pltpu.VMEM((tokens, HALF), BF16),
            pltpu.VMEM((tokens, HALF), BF16),
            pltpu.VMEM((tokens, HALF), BF16),
            pltpu.VMEM((HROW, DCOL), BF16),
            pltpu.VMEM((256, DCOL), BF16),
            pltpu.VMEM((128, DCOL), BF16),
            pltpu.VMEM((64, DCOL), BF16),
            pltpu.VMEM((128, DCOL), BF16),
            pltpu.VMEM((64, DCOL), BF16),
            pltpu.VMEM((64, DCOL), BF16),
            dma((16,)), dma((16,)),
            dma((NZ,)), dma((NZ,)),
            dma((16,)), dma((16,)),
            dma((16,)), dma((16,)),
            dma((NZ,)), dma((NZ,)),
            dma((16,)), dma((16,)),
            dma((16,)), dma((16,)),
            dma((12,)), dma((12,)),
            dma((28,)), dma((28,)),
            dma((7,)),
        ],
        compiler_params=pltpu.CompilerParams(
            collective_id=0, has_side_effects=True, vmem_limit_bytes=48 * 1024 * 1024),
    )(attn_out, cotangent, out_weight)


def solution(mesh):
    in_specs = (P(("outer", "dp"), None), P(("outer", "dp"), "tensor"), P("dp", "tensor"))
    out_specs = (P(("outer", "dp"), None), P("dp", "tensor"))
    return jax.shard_map(local, mesh=mesh, in_specs=in_specs, out_specs=out_specs, check_vma=False)
```

```python
import functools

import jax
import jax.numpy as jnp
from jax import lax
from jax.experimental import pallas as pl
from jax.experimental.pallas import tpu as pltpu
from jax.sharding import PartitionSpec as P

MESH = pl.DeviceIdType.MESH
F32, BF16 = jnp.float32, jnp.bfloat16
NZ = 8
BLOCK = 128
TOK = 128
DCOL = 2048
HROW = 512
HALF = 256
NCH = 4
CW = DCOL // NCH
CLIP = 2.5


def signs():
    row = lax.broadcasted_iota(jnp.int32, (BLOCK, BLOCK), 0)
    col = lax.broadcasted_iota(jnp.int32, (BLOCK, BLOCK), 1)
    common = row & col
    common = common ^ (common >> 4)
    common = common ^ (common >> 2)
    common = common ^ (common >> 1)
    return (1 - 2 * (common & 1)).astype(F32).astype(BF16)


def dot(a, b):
    return jnp.dot(a, b, preferred_element_type=F32)


def kernel(attn, cot, w, out, outw, COTIN, COT, WV, WRT, ACT, AT, PART, PSEND, PRECV, OSEND, WG, RS1, RS2, RSX, S2, SX, FIN,
           ring_s, ring_r, sib_s, sib_r, att_s, att_r, arl_s, arl_r, par_s, par_r, out_s, out_r, orl_s, orl_r,
           rs_s, rs_r, ag_s, ag_r, loc):
    outer, me, t = lax.axis_index("outer"), lax.axis_index("dp"), lax.axis_index("tensor")
    z, c = me // 2, me % 2
    y, xh = outer // 2, outer % 2
    sib = z * 2 + 1 - c
    b1 = (y % 2 + y // 2) % 2
    b2 = y // 2
    y1 = y + 1 - 2 * (y % 2)
    y3 = 3 - y
    factor = (TOK * 2 * NZ * 8) ** (-0.5)

    def remote(src, dst, ssem, rsem, where):
        return pltpu.make_async_remote_copy(
            src_ref=src, dst_ref=dst, send_sem=ssem, recv_sem=rsem, device_id=where, device_id_type=MESH)

    def zdev(k):
        return {"dp": k}

    peer = {"tensor": 1 - t}

    def zat(dz):
        return (z + dz + 2 * NZ) % NZ

    def rows(ref, at, count, unit=None):
        return ref.at[pl.ds(pl.multiple_of(at, unit or count), count), :]

    barrier = pltpu.get_barrier_semaphore()

    def greet(k, carry):
        pl.semaphore_signal(barrier, inc=1, device_id={"dp": (me + k) % (2 * NZ)}, device_id_type=MESH)
        return carry

    lax.fori_loop(1, 2 * NZ, greet, 0)
    pl.semaphore_signal(barrier, inc=1, device_id=peer, device_id_type=MESH)
    for where in (y1 * 2 + xh, y3 * 2 + xh, y * 2 + 1 - xh):
        pl.semaphore_signal(barrier, inc=1, device_id={"outer": where}, device_id_type=MESH)

    load_w = pltpu.make_async_copy(w, WV, loc.at[0])
    load_w.start()
    own_act = pltpu.make_async_copy(
        attn.at[:, pl.ds(pl.multiple_of(me * HROW, HROW), HROW)], rows(ACT, me * TOK, TOK), loc.at[1])
    own_act.start()

    load_cot = pltpu.make_async_copy(cot, COTIN, loc.at[3])
    load_cot.start()
    S = signs()
    load_cot.wait()
    for b in range(DCOL // BLOCK):
        k, inside = b * BLOCK // CW, b * BLOCK % CW
        turned = dot(COTIN[:, b * BLOCK:(b + 1) * BLOCK], S) * 0.125
        COT[k, pl.ds(pl.multiple_of(me * TOK, TOK), TOK), inside:inside + BLOCK] = turned.astype(BF16)

    pl.semaphore_wait(barrier, 2 * NZ - 1 + 4)

    def goes(direction, step, half):
        return step < 3 or direction == half

    def ring_block(direction, k, step, half, target_step):
        sgn = 1 - 2 * direction
        at = ((direction * NCH + k) * 4 + step) * 2 + half
        block = rows(COT.at[k], (zat(-sgn * target_step) * 2 + c) * TOK + half * 64, 64)
        return remote(block, block, ring_s.at[at], ring_r.at[at], zdev(zat(sgn) * 2 + c))

    def ring(direction, k, step, half):
        return ring_block(direction, k, step, half, step)

    def ring_in(direction, k, step, half):
        return ring_block(direction, k, step, half, step + 1)

    def sib_copy(k, dz, core):
        at = k * NZ + dz % NZ
        block = rows(COT.at[k], (zat(dz) * 2 + core) * TOK, TOK)
        return remote(block, block, sib_s.at[at], sib_r.at[at], zdev(sib))

    def other(k, dz):
        return zat((1 - 2 * (k // 2)) * dz) * 2 + k % 2

    def count(dz):
        return 2 if dz == NZ // 2 else 4

    def att_copy(to):
        src = attn.at[pl.ds(pl.multiple_of(t * 64, 64), 64), pl.ds(pl.multiple_of(to * HROW, HROW), HROW)]
        return remote(src, rows(ACT, me * TOK + t * 64, 64), att_s.at[to], att_r.at[me], zdev(to))

    def att_in(j):
        block = rows(ACT, j * TOK + t * 64, 64)
        return remote(block, block, att_s.at[j], att_r.at[j], zdev(j))

    def arl_copy(j):
        block = rows(ACT, j * TOK + t * 64, 64)
        return remote(block, block, arl_s.at[j], arl_r.at[j], peer)

    def arl_in(j):
        block = rows(ACT, j * TOK + (1 - t) * 64, 64)
        return remote(block, block, arl_s.at[j], arl_r.at[j], peer)

    def sib_att():
        return remote(attn.at[:, pl.ds(pl.multiple_of(sib * HROW, HROW), HROW)], rows(ACT, me * TOK, TOK),
                      att_s.at[sib], att_r.at[me], zdev(sib))

    def sib_att_in():
        block = rows(ACT, sib * TOK, TOK)
        return remote(block, block, att_s.at[sib], att_r.at[sib], zdev(sib))

    def over(dz, body):
        def step(k, carry):
            body(other(k, dz))
            return carry
        lax.fori_loop(0, count(dz), step, 0)

    def att_send(dz):
        over(dz, lambda j: att_copy(j).start())

    def att_relay(dz):
        def body(j):
            att_in(j).wait_recv()
            arl_copy(j).start()
        over(dz, body)

    def turn(j):
        AT[:, pl.ds(pl.multiple_of(j * TOK, TOK), TOK)] = ACT[pl.ds(pl.multiple_of(j * TOK, TOK), TOK), :].T

    def att_finish(dz):
        def body(j):
            arl_in(j).wait_recv()
            turn(j)
        over(dz, body)

    def par_copy(zz):
        return remote(rows(PSEND, zz * HALF, HALF), rows(PRECV, zz * HALF, HALF), par_s.at[zz], par_r.at[zz], peer)

    def process(zz):
        at = pl.ds(pl.multiple_of(zz * HALF, HALF), HALF)

        def half(which):
            columns = pl.ds(pl.multiple_of(which * HALF, HALF), HALF)
            return sum(dot(COT[k, at, :], WRT[k * CW:(k + 1) * CW, columns]) for k in range(NCH))

        PSEND[at, :] = half(1 - t).astype(BF16)
        par_copy(zz).start()
        PART[at, :] = half(t)

    def mine(j):
        return out.at[:, pl.ds(pl.multiple_of(j * HROW + t * HALF, HALF), HALF)]

    def theirs(j):
        return out.at[:, pl.ds(pl.multiple_of(j * HROW + (1 - t) * HALF, HALF), HALF)]

    def out_copy(to):
        return remote(rows(OSEND, to * TOK, TOK), mine(me), out_s.at[to], out_r.at[me], zdev(to))

    def out_in(j):
        return remote(mine(j), mine(j), out_s.at[j], out_r.at[j], zdev(j))

    def orl_copy(j, src=None):
        return remote(mine(j) if src is None else src, mine(j), orl_s.at[j], orl_r.at[j], peer)

    def orl_in(j):
        return remote(theirs(j), theirs(j), orl_s.at[j], orl_r.at[j], peer)

    own_out = pltpu.make_async_copy(rows(OSEND, me * TOK, TOK), mine(me), loc.at[2])

    def out_sum(zz):
        par_copy(zz).wait_recv()
        at = pl.ds(pl.multiple_of(zz * HALF, HALF), HALF)
        OSEND[at, :] = (PART[at, :] + PRECV[at, :].astype(F32)).astype(BF16)

    def out_stage(zz):
        out_sum(zz)
        out_copy(zz * 2).start()
        out_copy(zz * 2 + 1).start()

    def out_relay(dz):
        def body(j):
            out_in(j).wait_recv()
            orl_copy(j).start()
        over(dz, body)

    ones = jnp.ones((BLOCK, BLOCK), BF16)
    scale = factor * 8.0 * BLOCK ** (-0.5)

    def weight(k):
        def piece(n, carry):
            at = pl.multiple_of(n * HALF, HALF)
            acc = dot(AT[pl.ds(at, HALF), :], COT[k]) * scale
            clipped = []
            for b in range(CW // BLOCK):
                x = acc[:, b * BLOCK:(b + 1) * BLOCK]
                mean = dot((x * x).astype(BF16), ones) * (1.0 / BLOCK)
                limit = CLIP * jnp.sqrt(mean + 1e-6)
                clipped.append(jnp.clip(x, -limit, limit).astype(BF16))
            WG[pl.ds(pl.multiple_of(k * HROW + n * HALF, HALF), HALF), :] = jnp.concatenate(clipped, axis=1)
            return carry
        lax.fori_loop(0, HROW // HALF, piece, 0)

    def pick(half, a, b):
        return (1 - half) * a + half * b

    def place(i):
        half = i % 2
        p1, p2 = pick(half, y1, y3) * 2 + xh, pick(half, y3, y1) * 2 + xh
        return p1, p2, pick(half, b1, b2), pick(half, b2, b1), i * 256

    px = {"outer": y * 2 + 1 - xh}

    def ds16(at, n):
        return pl.ds(pl.multiple_of(at, 16), n)

    def rs1_copy(i):
        p1, p2, q1, q2, base = place(i)
        return remote(WG.at[ds16(base + (1 - q1) * 128, 128), :], RS1.at[ds16(i * 128, 128), :],
                      rs_s.at[i], rs_r.at[i], {"outer": p1})

    def rs2_copy(i):
        p1, p2, q1, q2, base = place(i)
        return remote(S2.at[ds16(i * 64, 64), :], RS2.at[ds16(i * 64, 64), :], rs_s.at[8 + i], rs_r.at[8 + i], {"outer": p2})

    def rsx_copy(i):
        return remote(SX.at[ds16(i * 32, 32), :], RSX.at[ds16(i * 32, 32), :], rs_s.at[16 + i], rs_r.at[16 + i], px)

    def combos(body, k):
        body(2 * k)
        body(2 * k + 1)

    def stage2(i):
        p1, p2, q1, q2, base = place(i)
        rs1_copy(i).wait_recv()
        off = (1 - q2) * 64
        S2[ds16(i * 64, 64), :] = (WG[ds16(base + q1 * 128 + off, 64), :].astype(F32)
                                   + RS1[ds16(i * 128 + off, 64), :].astype(F32)).astype(BF16)
        rs2_copy(i).start()

    def three(i, row):
        p1, p2, q1, q2, base = place(i)
        return (WG[ds16(base + q1 * 128 + q2 * 64 + row, 32), :].astype(F32)
                + RS1[ds16(i * 128 + q2 * 64 + row, 32), :].astype(F32)
                + RS2[ds16(i * 64 + row, 32), :].astype(F32))

    def stage3(i):
        rs2_copy(i).wait_recv()
        SX[ds16(i * 32, 32), :] = three(i, (1 - xh) * 32).astype(BF16)
        rsx_copy(i).start()

    def ag_row(i, f1, f2, fx):
        p1, p2, q1, q2, base = place(i)
        a = q1 if f1 == 0 else 1 - q1
        b = q2 if f2 == 0 else 1 - q2
        d = xh if fx == 0 else 1 - xh
        return outw.at[ds16(i % 2 * 256 + a * 128 + b * 64 + d * 32, 32), pl.ds(pl.multiple_of(i // 2 * CW, CW), CW)]

    KIND = ((0, 0, 0), (0, 0, 0), (0, 0, 0), (0, 0, 1), (0, 0, 1), (0, 1, 0), (0, 1, 1))
    FLIP = ((0, 0, 1), (0, 1, 0), (1, 0, 0), (0, 1, 1), (1, 0, 1), (1, 1, 0), (1, 1, 1))

    def ag_dev(i, kind):
        p1, p2, q1, q2, base = place(i)
        if kind == 0:
            return px
        return {"outer": p2 if kind in (1, 3) else p1}

    def ag_copy(i, kind, src=None):
        row = ag_row(i, *KIND[kind])
        return remote(row if src is None else src, row, ag_s.at[i * 7 + kind], ag_r.at[i * 7 + kind], ag_dev(i, kind))

    def ag_in(i, kind):
        row = ag_row(i, *FLIP[kind])
        return remote(row, row, ag_s.at[i * 7 + kind], ag_r.at[i * 7 + kind], ag_dev(i, kind))

    def own_fin(i):
        return pltpu.make_async_copy(FIN.at[ds16(i * 32, 32), :], ag_row(i, 0, 0, 0), loc.at[4 + i])

    def stage4(i):
        rsx_copy(i).wait_recv()
        total = three(i, xh * 32) + RSX[ds16(i * 32, 32), :].astype(F32)
        high = total.astype(BF16)
        low = (total - high.astype(F32)).astype(BF16)
        both = jnp.concatenate([high, low], axis=0)
        pieces = []
        for b in range(CW // BLOCK):
            r = dot(both[:, b * BLOCK:(b + 1) * BLOCK], S)
            pieces.append(((r[:32] + r[32:]) * (BLOCK ** (-0.5))).astype(BF16))
        FIN[ds16(i * 32, 32), :] = jnp.concatenate(pieces, axis=1)
        for kind in range(3):
            ag_copy(i, kind, FIN.at[ds16(i * 32, 32), :]).start()
        own_fin(i).start()

    def stage5(i):
        ag_in(i, 0).wait_recv()
        ag_copy(i, 3).start()
        ag_copy(i, 4).start()

    def stage6(i):
        ag_in(i, 1).wait_recv()
        ag_copy(i, 5).start()
        ag_in(i, 3).wait_recv()
        ag_copy(i, 6).start()

    def stage7(i):
        for kind in (2, 4, 5, 6):
            ag_in(i, kind).wait_recv()

    def send_ring(k, step):
        for half in range(2):
            for direction in range(2):
                if step and goes(direction, step - 1, half):
                    ring_in(direction, k, step - 1, half).wait_recv()
                if step < 4 and goes(direction, step, half):
                    ring(direction, k, step, half).start()
        for dz in ((0,) if step == 0 else (4,) if step == 4 else (-step, step)):
            sib_copy(k, dz, c).start()

    def sib_wait(k, step):
        for dz in ((0,) if step == 0 else (4,) if step == 4 else (-step, step)):
            sib_copy(k, dz, 1 - c).wait_recv()

    SKEW = (0, 0, 3, 3)

    def slot_items(slot):
        return [(k, slot - SKEW[k]) for k in range(NCH) if 0 <= slot - SKEW[k] <= 4]

    ORDER = (4, 3, 2, 1)

    def reduce_stage(k):
        for i in (2 * k, 2 * k + 1):
            rs1_copy(i).start()

    def chain(slot, first):
        for k in range(NCH):
            a = slot - first[k]
            if 1 <= a <= 5:
                combos((stage2, stage3, stage4, stage5, stage6)[a - 1], k)

    FIRST = tuple(max(5, at + 4) for at in SKEW)
    END = SKEW[-1] + 4

    for slot in range(END + 1):
        for k, step in slot_items(slot):
            send_ring(k, step)
        if slot < 4:
            att_send(ORDER[slot])
        if slot == 0:
            sib_att().start()
            load_w.wait()
            for b in range(DCOL // BLOCK):
                part = slice(b * BLOCK, (b + 1) * BLOCK)
                turned = lax.dot_general(S, WV[:, part], (((0,), (1,)), ((), ())), preferred_element_type=F32)
                WRT[part, :] = (turned * 0.0625).astype(BF16)
            own_act.wait()
            turn(me)
            sib_att_in().wait_recv()
            turn(sib)
        if 1 <= slot <= 4:
            att_relay(ORDER[slot - 1])
        if 2 <= slot <= 5:
            att_finish(ORDER[slot - 2])
        if slot < END:
            chain(slot, FIRST)
        for k, step in slot_items(slot):
            sib_wait(k, step)
        for k in range(NCH):
            if slot == FIRST[k]:
                weight(k)
                reduce_stage(k)
        if slot == END:
            chain(slot, FIRST)
        if slot == END - 3:
            process(z)
        if slot >= END - 3:
            step = slot - END + 4
            for dz in ((4,) if step == 4 else (-step, step)):
                process(zat(dz))
        if slot == END - 2:
            out_sum(z)
            own_out.start()
            out_copy(sib).start()
            orl_copy(me, rows(OSEND, me * TOK, TOK)).start()
        if slot == END - 1:
            out_stage(zat(1))
            out_stage(zat(-1))
        if slot == END:
            for dz in (2, -2, 3, -3):
                out_stage(zat(dz))
            out_in(sib).wait_recv()
            orl_copy(sib).start()

    chain(END + 1, FIRST)
    out_stage(zat(4))
    out_relay(1)
    chain(END + 2, FIRST)
    chain(END + 3, FIRST)
    out_relay(2)
    chain(END + 4, FIRST)
    chain(END + 5, FIRST)
    out_relay(3)
    out_relay(4)
    for k in range(NCH):
        combos(stage7, k)

    def all_j(body):
        def step(k, carry):
            body(k)
            return carry
        lax.fori_loop(0, 2 * NZ, step, 0)

    all_j(lambda j: orl_in(j).wait_recv())
    own_out.wait()
    for k in range(NCH):
        for direction in range(2):
            for step in range(4):
                for half in range(2):
                    if goes(direction, step, half):
                        ring(direction, k, step, half).wait_send()
        for dz in range(NZ):
            sib_copy(k, dz, c).wait_send()
    sib_att().wait_send()
    out_copy(sib).wait_send()
    for dz in range(1, 5):
        def body(j):
            att_copy(j).wait_send()
            arl_copy(j).wait_send()
            out_copy(j).wait_send()
        over(dz, body)
    all_j(lambda j: orl_copy(j).wait_send())

    def parts(zz, carry):
        par_copy(zz).wait_send()
        return carry

    lax.fori_loop(0, NZ, parts, 0)

    def sums(i):
        rs1_copy(i).wait_send()
        rs2_copy(i).wait_send()
        rsx_copy(i).wait_send()
        for kind in range(7):
            ag_copy(i, kind).wait_send()
        own_fin(i).wait()

    lax.fori_loop(0, 2 * NCH, lambda i, carry: (sums(i), carry)[1], 0)


def local(attn_out, cotangent, out_weight):
    hbm = pl.BlockSpec(memory_space=pl.ANY)
    dma = pltpu.SemaphoreType.DMA
    tokens = TOK * 2 * NZ
    return pl.pallas_call(
        kernel,
        out_shape=(jax.ShapeDtypeStruct(attn_out.shape, BF16), jax.ShapeDtypeStruct(out_weight.shape, BF16)),
        in_specs=[hbm, hbm, hbm],
        out_specs=(hbm, hbm),
        scratch_shapes=[
            pltpu.VMEM((TOK, DCOL), BF16),
            pltpu.VMEM((NCH, tokens, CW), BF16),
            pltpu.VMEM((HROW, DCOL), BF16),
            pltpu.VMEM((DCOL, HROW), BF16),
            pltpu.VMEM((tokens, HROW), BF16),
            pltpu.VMEM((HROW, tokens), BF16),
            pltpu.VMEM((tokens, HALF), F32),
            pltpu.VMEM((tokens, HALF), BF16),
            pltpu.VMEM((tokens, HALF), BF16),
            pltpu.VMEM((tokens, HALF), BF16),
            pltpu.VMEM((NCH * HROW, CW), BF16),
            pltpu.VMEM((1024, CW), BF16),
            pltpu.VMEM((512, CW), BF16),
            pltpu.VMEM((256, CW), BF16),
            pltpu.VMEM((512, CW), BF16),
            pltpu.VMEM((256, CW), BF16),
            pltpu.VMEM((256, CW), BF16),
            dma((64,)), dma((64,)),
            dma((NCH * NZ,)), dma((NCH * NZ,)),
            dma((16,)), dma((16,)),
            dma((16,)), dma((16,)),
            dma((NZ,)), dma((NZ,)),
            dma((16,)), dma((16,)),
            dma((16,)), dma((16,)),
            dma((24,)), dma((24,)),
            dma((56,)), dma((56,)),
            dma((12,)),
        ],
        compiler_params=pltpu.CompilerParams(
            collective_id=0, has_side_effects=True, vmem_limit_bytes=48 * 1024 * 1024),
    )(attn_out, cotangent, out_weight)


def solution(mesh):
    in_specs = (P(("outer", "dp"), None), P(("outer", "dp"), "tensor"), P("dp", "tensor"))
    out_specs = (P(("outer", "dp"), None), P("dp", "tensor"))
    return jax.shard_map(local, mesh=mesh, in_specs=in_specs, out_specs=out_specs, check_vma=False)
```

```python
import functools

import jax
import jax.numpy as jnp
from jax import lax
from jax.experimental import pallas as pl
from jax.experimental.pallas import tpu as pltpu
from jax.sharding import PartitionSpec as P

MESH = pl.DeviceIdType.MESH
F32, BF16 = jnp.float32, jnp.bfloat16
NZ = 8
BLOCK = 128
TOK = 128
DCOL = 2048
HROW = 512
HALF = 256
NCH = 4
CW = DCOL // NCH
CLIP = 2.5


def signs():
    row = lax.broadcasted_iota(jnp.int32, (BLOCK, BLOCK), 0)
    col = lax.broadcasted_iota(jnp.int32, (BLOCK, BLOCK), 1)
    common = row & col
    common = common ^ (common >> 4)
    common = common ^ (common >> 2)
    common = common ^ (common >> 1)
    return (1 - 2 * (common & 1)).astype(F32).astype(BF16)


def dot(a, b):
    return jnp.dot(a, b, preferred_element_type=F32)


def kernel(attn, cot, w, out, outw, COTIN, COT, WV, WRT, ACT, AT, PART, PSEND, PRECV, OSEND, WG, RS1, RS2, RSX, S2, SX, FIN,
           ring_s, ring_r, sib_s, sib_r, att_s, att_r, arl_s, arl_r, par_s, par_r, out_s, out_r, orl_s, orl_r,
           rs_s, rs_r, ag_s, ag_r, loc):
    outer, me, t = lax.axis_index("outer"), lax.axis_index("dp"), lax.axis_index("tensor")
    z, c = me // 2, me % 2
    y, xh = outer // 2, outer % 2
    sib = z * 2 + 1 - c
    b1 = (y % 2 + y // 2) % 2
    b2 = y // 2
    y1 = y + 1 - 2 * (y % 2)
    y3 = 3 - y
    factor = (TOK * 2 * NZ * 8) ** (-0.5)

    def remote(src, dst, ssem, rsem, where):
        return pltpu.make_async_remote_copy(
            src_ref=src, dst_ref=dst, send_sem=ssem, recv_sem=rsem, device_id=where, device_id_type=MESH)

    def zdev(k):
        return {"dp": k}

    peer = {"tensor": 1 - t}

    def zat(dz):
        return (z + dz + 2 * NZ) % NZ

    def rows(ref, at, count, unit=None):
        return ref.at[pl.ds(pl.multiple_of(at, unit or count), count), :]

    barrier = pltpu.get_barrier_semaphore()

    def greet(k, carry):
        pl.semaphore_signal(barrier, inc=1, device_id={"dp": (me + k) % (2 * NZ)}, device_id_type=MESH)
        return carry

    lax.fori_loop(1, 2 * NZ, greet, 0)
    pl.semaphore_signal(barrier, inc=1, device_id=peer, device_id_type=MESH)
    for where in (y1 * 2 + xh, y3 * 2 + xh, y * 2 + 1 - xh):
        pl.semaphore_signal(barrier, inc=1, device_id={"outer": where}, device_id_type=MESH)

    load_w = pltpu.make_async_copy(w, WV, loc.at[0])
    load_w.start()
    own_act = pltpu.make_async_copy(
        attn.at[:, pl.ds(pl.multiple_of(me * HROW, HROW), HROW)], rows(ACT, me * TOK, TOK), loc.at[1])
    own_act.start()

    load_cot = pltpu.make_async_copy(cot, COTIN, loc.at[3])
    load_cot.start()
    S = signs()
    load_cot.wait()
    for b in range(DCOL // BLOCK):
        k, inside = b * BLOCK // CW, b * BLOCK % CW
        turned = dot(COTIN[:, b * BLOCK:(b + 1) * BLOCK], S) * 0.125
        COT[k, pl.ds(pl.multiple_of(me * TOK, TOK), TOK), inside:inside + BLOCK] = turned.astype(BF16)

    pl.semaphore_wait(barrier, 2 * NZ - 1 + 4)

    def goes(direction, step, half):
        return step < 3 or direction == half

    def ring_block(direction, k, step, half, target_step):
        sgn = 1 - 2 * direction
        at = ((direction * NCH + k) * 4 + step) * 2 + half
        block = rows(COT.at[k], (zat(-sgn * target_step) * 2 + c) * TOK + half * 64, 64)
        return remote(block, block, ring_s.at[at], ring_r.at[at], zdev(zat(sgn) * 2 + c))

    def ring(direction, k, step, half):
        return ring_block(direction, k, step, half, step)

    def ring_in(direction, k, step, half):
        return ring_block(direction, k, step, half, step + 1)

    def sib_copy(k, dz, core):
        at = k * NZ + dz % NZ
        block = rows(COT.at[k], (zat(dz) * 2 + core) * TOK, TOK)
        return remote(block, block, sib_s.at[at], sib_r.at[at], zdev(sib))

    def other(k, dz):
        return zat((1 - 2 * (k // 2)) * dz) * 2 + k % 2

    def count(dz):
        return 2 if dz == NZ // 2 else 4

    def att_copy(to):
        src = attn.at[pl.ds(pl.multiple_of(t * 64, 64), 64), pl.ds(pl.multiple_of(to * HROW, HROW), HROW)]
        return remote(src, rows(ACT, me * TOK + t * 64, 64), att_s.at[to], att_r.at[me], zdev(to))

    def att_in(j):
        block = rows(ACT, j * TOK + t * 64, 64)
        return remote(block, block, att_s.at[j], att_r.at[j], zdev(j))

    def arl_copy(j):
        block = rows(ACT, j * TOK + t * 64, 64)
        return remote(block, block, arl_s.at[j], arl_r.at[j], peer)

    def arl_in(j):
        block = rows(ACT, j * TOK + (1 - t) * 64, 64)
        return remote(block, block, arl_s.at[j], arl_r.at[j], peer)

    def sib_att():
        return remote(attn.at[:, pl.ds(pl.multiple_of(sib * HROW, HROW), HROW)], rows(ACT, me * TOK, TOK),
                      att_s.at[sib], att_r.at[me], zdev(sib))

    def sib_att_in():
        block = rows(ACT, sib * TOK, TOK)
        return remote(block, block, att_s.at[sib], att_r.at[sib], zdev(sib))

    def over(dz, body):
        def step(k, carry):
            body(other(k, dz))
            return carry
        lax.fori_loop(0, count(dz), step, 0)

    def att_send(dz):
        over(dz, lambda j: att_copy(j).start())

    def att_relay(dz):
        def body(j):
            att_in(j).wait_recv()
            arl_copy(j).start()
        over(dz, body)

    def turn(j):
        AT[:, pl.ds(pl.multiple_of(j * TOK, TOK), TOK)] = ACT[pl.ds(pl.multiple_of(j * TOK, TOK), TOK), :].T

    def att_finish(dz):
        def body(j):
            arl_in(j).wait_recv()
            turn(j)
        over(dz, body)

    def par_copy(zz):
        return remote(rows(PSEND, zz * HALF, HALF), rows(PRECV, zz * HALF, HALF), par_s.at[zz], par_r.at[zz], peer)

    def process(zz):
        at = pl.ds(pl.multiple_of(zz * HALF, HALF), HALF)

        def half(which):
            columns = pl.ds(pl.multiple_of(which * HALF, HALF), HALF)
            return sum(dot(COT[k, at, :], WRT[k * CW:(k + 1) * CW, columns]) for k in range(NCH))

        PSEND[at, :] = half(1 - t).astype(BF16)
        par_copy(zz).start()
        PART[at, :] = half(t)

    def mine(j):
        return out.at[:, pl.ds(pl.multiple_of(j * HROW + t * HALF, HALF), HALF)]

    def theirs(j):
        return out.at[:, pl.ds(pl.multiple_of(j * HROW + (1 - t) * HALF, HALF), HALF)]

    def out_copy(to):
        return remote(rows(OSEND, to * TOK, TOK), mine(me), out_s.at[to], out_r.at[me], zdev(to))

    def out_in(j):
        return remote(mine(j), mine(j), out_s.at[j], out_r.at[j], zdev(j))

    def orl_copy(j, src=None):
        return remote(mine(j) if src is None else src, mine(j), orl_s.at[j], orl_r.at[j], peer)

    def orl_in(j):
        return remote(theirs(j), theirs(j), orl_s.at[j], orl_r.at[j], peer)

    own_out = pltpu.make_async_copy(rows(OSEND, me * TOK, TOK), mine(me), loc.at[2])

    def out_sum(zz):
        par_copy(zz).wait_recv()
        at = pl.ds(pl.multiple_of(zz * HALF, HALF), HALF)
        OSEND[at, :] = (PART[at, :] + PRECV[at, :].astype(F32)).astype(BF16)

    def out_stage(zz):
        out_sum(zz)
        out_copy(zz * 2).start()
        out_copy(zz * 2 + 1).start()

    def out_relay(dz):
        def body(j):
            out_in(j).wait_recv()
            orl_copy(j).start()
        over(dz, body)

    ones = jnp.ones((BLOCK, BLOCK), BF16)
    scale = factor * 8.0 * BLOCK ** (-0.5)

    def weight(k):
        def piece(n, carry):
            at = pl.multiple_of(n * HALF, HALF)
            acc = dot(AT[pl.ds(at, HALF), :], COT[k]) * scale
            clipped = []
            for b in range(CW // BLOCK):
                x = acc[:, b * BLOCK:(b + 1) * BLOCK]
                mean = dot((x * x).astype(BF16), ones) * (1.0 / BLOCK)
                limit = CLIP * jnp.sqrt(mean + 1e-6)
                clipped.append(jnp.clip(x, -limit, limit).astype(BF16))
            WG[pl.ds(pl.multiple_of(k * HROW + n * HALF, HALF), HALF), :] = jnp.concatenate(clipped, axis=1)
            return carry
        lax.fori_loop(0, HROW // HALF, piece, 0)

    def pick(half, a, b):
        return (1 - half) * a + half * b

    def place(i):
        half = i % 2
        p1, p2 = pick(half, y1, y3) * 2 + xh, pick(half, y3, y1) * 2 + xh
        return p1, p2, pick(half, b1, b2), pick(half, b2, b1), i * 256

    px = {"outer": y * 2 + 1 - xh}

    def ds16(at, n):
        return pl.ds(pl.multiple_of(at, 16), n)

    def rs1_copy(i):
        p1, p2, q1, q2, base = place(i)
        return remote(WG.at[ds16(base + (1 - q1) * 128, 128), :], RS1.at[ds16(i * 128, 128), :],
                      rs_s.at[i], rs_r.at[i], {"outer": p1})

    def rs2_copy(i):
        p1, p2, q1, q2, base = place(i)
        return remote(S2.at[ds16(i * 64, 64), :], RS2.at[ds16(i * 64, 64), :], rs_s.at[8 + i], rs_r.at[8 + i], {"outer": p2})

    def rsx_copy(i):
        return remote(SX.at[ds16(i * 64, 64), :], RSX.at[ds16(i * 64, 64), :], rs_s.at[16 + i], rs_r.at[16 + i], px)

    def combos(body, k):
        body(2 * k)
        body(2 * k + 1)

    def stage2(i):
        p1, p2, q1, q2, base = place(i)
        rs1_copy(i).wait_recv()
        off = (1 - q2) * 64
        S2[ds16(i * 64, 64), :] = (WG[ds16(base + q1 * 128 + off, 64), :].astype(F32)
                                   + RS1[ds16(i * 128 + off, 64), :].astype(F32)).astype(BF16)
        rs2_copy(i).start()

    def stage3(i):
        p1, p2, q1, q2, base = place(i)
        rs2_copy(i).wait_recv()
        SX[ds16(i * 64, 64), :] = (WG[ds16(base + q1 * 128 + q2 * 64, 64), :].astype(F32)
                                   + RS1[ds16(i * 128 + q2 * 64, 64), :].astype(F32)
                                   + RS2[ds16(i * 64, 64), :].astype(F32)).astype(BF16)
        rsx_copy(i).start()

    def ag_row(i, f1, f2):
        p1, p2, q1, q2, base = place(i)
        a = q1 if f1 == 0 else 1 - q1
        b = q2 if f2 == 0 else 1 - q2
        return outw.at[ds16(i % 2 * 256 + a * 128 + b * 64, 64), pl.ds(pl.multiple_of(i // 2 * CW, CW), CW)]

    KIND = ((0, 0), (0, 0), (0, 1))
    FLIP = ((0, 1), (1, 0), (1, 1))

    def ag_copy(i, kind, src=None):
        p1, p2, q1, q2, base = place(i)
        row = ag_row(i, *KIND[kind])
        return remote(row if src is None else src, row, ag_s.at[i * 3 + kind], ag_r.at[i * 3 + kind],
                      {"outer": p2 if kind == 0 else p1})

    def ag_in(i, kind):
        p1, p2, q1, q2, base = place(i)
        row = ag_row(i, *FLIP[kind])
        return remote(row, row, ag_s.at[i * 3 + kind], ag_r.at[i * 3 + kind], {"outer": p2 if kind == 0 else p1})

    def own_fin(i):
        return pltpu.make_async_copy(FIN.at[ds16(i * 64, 64), :], ag_row(i, 0, 0), loc.at[4 + i])

    def stage4(i):
        rsx_copy(i).wait_recv()
        total = SX[ds16(i * 64, 64), :].astype(F32) + RSX[ds16(i * 64, 64), :].astype(F32)
        high = total.astype(BF16)
        low = (total - high.astype(F32)).astype(BF16)
        both = jnp.concatenate([high, low], axis=0)
        pieces = []
        for b in range(CW // BLOCK):
            r = dot(both[:, b * BLOCK:(b + 1) * BLOCK], S)
            pieces.append(((r[:64] + r[64:]) * (BLOCK ** (-0.5))).astype(BF16))
        FIN[ds16(i * 64, 64), :] = jnp.concatenate(pieces, axis=1)
        for kind in range(2):
            ag_copy(i, kind, FIN.at[ds16(i * 64, 64), :]).start()
        own_fin(i).start()

    def stage5(i):
        ag_in(i, 0).wait_recv()
        ag_copy(i, 2).start()

    def stage7(i):
        for kind in (1, 2):
            ag_in(i, kind).wait_recv()

    def send_ring(k, step):
        for half in range(2):
            for direction in range(2):
                if step and goes(direction, step - 1, half):
                    ring_in(direction, k, step - 1, half).wait_recv()
                if step < 4 and goes(direction, step, half):
                    ring(direction, k, step, half).start()
        for dz in ((0,) if step == 0 else (4,) if step == 4 else (-step, step)):
            sib_copy(k, dz, c).start()

    def sib_wait(k, step):
        for dz in ((0,) if step == 0 else (4,) if step == 4 else (-step, step)):
            sib_copy(k, dz, 1 - c).wait_recv()

    SKEW = (0, 0, 3, 3)

    def slot_items(slot):
        return [(k, slot - SKEW[k]) for k in range(NCH) if 0 <= slot - SKEW[k] <= 4]

    SENDS = {0: (4,), 1: (3, 2), 2: (1,)}

    def reduce_stage(k):
        for i in (2 * k, 2 * k + 1):
            rs1_copy(i).start()

    def chain(slot, first):
        for k in range(NCH):
            a = slot - first[k]
            if 1 <= a <= 4:
                combos((stage2, stage3, stage4, stage5)[a - 1], k)

    FIRST = (4, 5, 7, 7)
    END = SKEW[-1] + 4
    SUMS = (END - 2, END - 1, END, END)

    for slot in range(END + 1):
        for k, step in slot_items(slot):
            send_ring(k, step)
        for dz in SENDS.get(slot, ()):
            att_send(dz)
        if slot == 0:
            sib_att().start()
            load_w.wait()
            for b in range(DCOL // BLOCK):
                part = slice(b * BLOCK, (b + 1) * BLOCK)
                turned = lax.dot_general(S, WV[:, part], (((0,), (1,)), ((), ())), preferred_element_type=F32)
                WRT[part, :] = (turned * 0.0625).astype(BF16)
            own_act.wait()
            turn(me)
            sib_att_in().wait_recv()
            turn(sib)
        for dz in SENDS.get(slot - 1, ()):
            att_relay(dz)
        for dz in SENDS.get(slot - 2, ()):
            att_finish(dz)
        if slot < END:
            chain(slot, SUMS)
        for k, step in slot_items(slot):
            sib_wait(k, step)
        if slot == END:
            out_stage(zat(2))
            out_stage(zat(-2))
        for k in range(NCH):
            if slot == FIRST[k]:
                weight(k)
                reduce_stage(k)
        if slot == END:
            chain(slot, SUMS)
        if slot == END - 3:
            process(z)
        if slot >= END - 3:
            step = slot - END + 4
            for dz in ((4,) if step == 4 else (-step, step)):
                process(zat(dz))
        if slot == END - 2:
            out_sum(z)
            own_out.start()
            out_copy(sib).start()
            orl_copy(me, rows(OSEND, me * TOK, TOK)).start()
        if slot == END - 1:
            out_stage(zat(1))
            out_stage(zat(-1))
        if slot == END:
            for dz in (3, -3):
                out_stage(zat(dz))
            out_in(sib).wait_recv()
            orl_copy(sib).start()

    out_stage(zat(4))
    out_relay(1)
    chain(END + 1, SUMS)
    out_relay(2)
    for k in range(NCH):
        for direction in range(2):
            for step in range(4):
                for half in range(2):
                    if goes(direction, step, half):
                        ring(direction, k, step, half).wait_send()
        for dz in range(NZ):
            sib_copy(k, dz, c).wait_send()
    sib_att().wait_send()

    def sent(j):
        att_copy(j).wait_send()
        arl_copy(j).wait_send()

    for dz in range(1, 5):
        over(dz, sent)

    def parts(zz, carry):
        par_copy(zz).wait_send()
        return carry

    lax.fori_loop(0, NZ, parts, 0)

    chain(END + 2, SUMS)
    out_relay(3)
    chain(END + 3, SUMS)
    out_relay(4)
    chain(END + 4, SUMS)
    for k in range(NCH):
        combos(stage7, k)

    def all_j(body):
        def step(k, carry):
            body(k)
            return carry
        lax.fori_loop(0, 2 * NZ, step, 0)

    all_j(lambda j: orl_in(j).wait_recv())
    own_out.wait()
    out_copy(sib).wait_send()
    for dz in range(1, 5):
        def body(j):
            out_copy(j).wait_send()
        over(dz, body)
    all_j(lambda j: orl_copy(j).wait_send())

    def sums(i):
        rs1_copy(i).wait_send()
        rs2_copy(i).wait_send()
        rsx_copy(i).wait_send()
        for kind in range(3):
            ag_copy(i, kind).wait_send()
        own_fin(i).wait()

    lax.fori_loop(0, 2 * NCH, lambda i, carry: (sums(i), carry)[1], 0)


def local(attn_out, cotangent, out_weight):
    hbm = pl.BlockSpec(memory_space=pl.ANY)
    dma = pltpu.SemaphoreType.DMA
    tokens = TOK * 2 * NZ
    return pl.pallas_call(
        kernel,
        out_shape=(jax.ShapeDtypeStruct(attn_out.shape, BF16), jax.ShapeDtypeStruct(out_weight.shape, BF16)),
        in_specs=[hbm, hbm, hbm],
        out_specs=(hbm, hbm),
        scratch_shapes=[
            pltpu.VMEM((TOK, DCOL), BF16),
            pltpu.VMEM((NCH, tokens, CW), BF16),
            pltpu.VMEM((HROW, DCOL), BF16),
            pltpu.VMEM((DCOL, HROW), BF16),
            pltpu.VMEM((tokens, HROW), BF16),
            pltpu.VMEM((HROW, tokens), BF16),
            pltpu.VMEM((tokens, HALF), F32),
            pltpu.VMEM((tokens, HALF), BF16),
            pltpu.VMEM((tokens, HALF), BF16),
            pltpu.VMEM((tokens, HALF), BF16),
            pltpu.VMEM((NCH * HROW, CW), BF16),
            pltpu.VMEM((1024, CW), BF16),
            pltpu.VMEM((512, CW), BF16),
            pltpu.VMEM((512, CW), BF16),
            pltpu.VMEM((512, CW), BF16),
            pltpu.VMEM((512, CW), BF16),
            pltpu.VMEM((512, CW), BF16),
            dma((64,)), dma((64,)),
            dma((NCH * NZ,)), dma((NCH * NZ,)),
            dma((16,)), dma((16,)),
            dma((16,)), dma((16,)),
            dma((NZ,)), dma((NZ,)),
            dma((16,)), dma((16,)),
            dma((16,)), dma((16,)),
            dma((24,)), dma((24,)),
            dma((24,)), dma((24,)),
            dma((12,)),
        ],
        compiler_params=pltpu.CompilerParams(
            collective_id=0, has_side_effects=True, vmem_limit_bytes=48 * 1024 * 1024),
    )(attn_out, cotangent, out_weight)


def solution(mesh):
    in_specs = (P(("outer", "dp"), None), P(("outer", "dp"), "tensor"), P("dp", "tensor"))
    out_specs = (P(("outer", "dp"), None), P("dp", "tensor"))
    return jax.shard_map(local, mesh=mesh, in_specs=in_specs, out_specs=out_specs, check_vma=False)
```

```python
import functools

import jax
import jax.numpy as jnp
from jax import lax
from jax.experimental import pallas as pl
from jax.experimental.pallas import tpu as pltpu
from jax.sharding import PartitionSpec as P

MESH = pl.DeviceIdType.MESH
F32, BF16 = jnp.float32, jnp.bfloat16
NZ = 8
BLOCK = 128
TOK = 128
DCOL = 2048
HROW = 512
HALF = 256
NCH = 4
CW = DCOL // NCH
CLIP = 2.5


def signs():
    row = lax.broadcasted_iota(jnp.int32, (BLOCK, BLOCK), 0)
    col = lax.broadcasted_iota(jnp.int32, (BLOCK, BLOCK), 1)
    common = row & col
    common = common ^ (common >> 4)
    common = common ^ (common >> 2)
    common = common ^ (common >> 1)
    return (1 - 2 * (common & 1)).astype(F32).astype(BF16)


def dot(a, b):
    return jnp.dot(a, b, preferred_element_type=F32)


def kernel(attn, cot, w, out, outw, COTIN, COT, WV, WRT, ACT, AT, PART, PSEND, PRECV, OSEND, WG, RS1, RS2, RSX, S2, SX, FIN,
           ring_s, ring_r, sib_s, sib_r, att_s, att_r, arl_s, arl_r, par_s, par_r, out_s, out_r, orl_s, orl_r,
           rs_s, rs_r, ag_s, ag_r, loc):
    outer, me, t = lax.axis_index("outer"), lax.axis_index("dp"), lax.axis_index("tensor")
    z, c = me // 2, me % 2
    y, xh = outer // 2, outer % 2
    sib = z * 2 + 1 - c
    b1 = (y % 2 + y // 2) % 2
    b2 = y // 2
    y1 = y + 1 - 2 * (y % 2)
    y3 = 3 - y
    factor = (TOK * 2 * NZ * 8) ** (-0.5)

    def remote(src, dst, ssem, rsem, where):
        return pltpu.make_async_remote_copy(
            src_ref=src, dst_ref=dst, send_sem=ssem, recv_sem=rsem, device_id=where, device_id_type=MESH)

    def zdev(k):
        return {"dp": k}

    peer = {"tensor": 1 - t}

    def zat(dz):
        return (z + dz + 2 * NZ) % NZ

    def rows(ref, at, count, unit=None):
        return ref.at[pl.ds(pl.multiple_of(at, unit or count), count), :]

    barrier = pltpu.get_barrier_semaphore()

    def greet(k, carry):
        pl.semaphore_signal(barrier, inc=1, device_id={"dp": (me + k) % (2 * NZ)}, device_id_type=MESH)
        return carry

    lax.fori_loop(1, 2 * NZ, greet, 0)
    pl.semaphore_signal(barrier, inc=1, device_id=peer, device_id_type=MESH)
    for where in (y1 * 2 + xh, y3 * 2 + xh, y * 2 + 1 - xh):
        pl.semaphore_signal(barrier, inc=1, device_id={"outer": where}, device_id_type=MESH)

    load_w = pltpu.make_async_copy(w, WV, loc.at[0])
    load_w.start()
    own_act = pltpu.make_async_copy(
        attn.at[:, pl.ds(pl.multiple_of(me * HROW, HROW), HROW)], rows(ACT, me * TOK, TOK), loc.at[1])
    own_act.start()

    load_cot = pltpu.make_async_copy(cot, COTIN, loc.at[3])
    load_cot.start()
    S = signs()
    load_cot.wait()
    for b in range(DCOL // BLOCK):
        k, inside = b * BLOCK // CW, b * BLOCK % CW
        turned = dot(COTIN[:, b * BLOCK:(b + 1) * BLOCK], S) * 0.125
        COT[k, pl.ds(pl.multiple_of(me * TOK, TOK), TOK), inside:inside + BLOCK] = turned.astype(BF16)

    pl.semaphore_wait(barrier, 2 * NZ - 1 + 4)

    def goes(direction, step, half):
        return step < 3 or direction == half

    def ring_block(direction, k, step, half, target_step):
        sgn = 1 - 2 * direction
        at = ((direction * NCH + k) * 4 + step) * 2 + half
        block = rows(COT.at[k], (zat(-sgn * target_step) * 2 + c) * TOK + half * 64, 64)
        return remote(block, block, ring_s.at[at], ring_r.at[at], zdev(zat(sgn) * 2 + c))

    def ring(direction, k, step, half):
        return ring_block(direction, k, step, half, step)

    def ring_in(direction, k, step, half):
        return ring_block(direction, k, step, half, step + 1)

    def sib_copy(k, dz, core):
        at = k * NZ + dz % NZ
        block = rows(COT.at[k], (zat(dz) * 2 + core) * TOK, TOK)
        return remote(block, block, sib_s.at[at], sib_r.at[at], zdev(sib))

    def other(k, dz):
        return zat((1 - 2 * (k // 2)) * dz) * 2 + k % 2

    def count(dz):
        return 2 if dz == NZ // 2 else 4

    def att_copy(to):
        src = attn.at[pl.ds(pl.multiple_of(t * 64, 64), 64), pl.ds(pl.multiple_of(to * HROW, HROW), HROW)]
        return remote(src, rows(ACT, me * TOK + t * 64, 64), att_s.at[to], att_r.at[me], zdev(to))

    def att_in(j):
        block = rows(ACT, j * TOK + t * 64, 64)
        return remote(block, block, att_s.at[j], att_r.at[j], zdev(j))

    def arl_copy(j):
        block = rows(ACT, j * TOK + t * 64, 64)
        return remote(block, block, arl_s.at[j], arl_r.at[j], peer)

    def arl_in(j):
        block = rows(ACT, j * TOK + (1 - t) * 64, 64)
        return remote(block, block, arl_s.at[j], arl_r.at[j], peer)

    def sib_att():
        return remote(attn.at[:, pl.ds(pl.multiple_of(sib * HROW, HROW), HROW)], rows(ACT, me * TOK, TOK),
                      att_s.at[sib], att_r.at[me], zdev(sib))

    def sib_att_in():
        block = rows(ACT, sib * TOK, TOK)
        return remote(block, block, att_s.at[sib], att_r.at[sib], zdev(sib))

    def over(dz, body):
        def step(k, carry):
            body(other(k, dz))
            return carry
        lax.fori_loop(0, count(dz), step, 0)

    def att_send(dz):
        over(dz, lambda j: att_copy(j).start())

    def att_relay(dz):
        def body(j):
            att_in(j).wait_recv()
            arl_copy(j).start()
        over(dz, body)

    def turn(j):
        AT[:, pl.ds(pl.multiple_of(j * TOK, TOK), TOK)] = ACT[pl.ds(pl.multiple_of(j * TOK, TOK), TOK), :].T

    def att_finish(dz):
        def body(j):
            arl_in(j).wait_recv()
            turn(j)
        over(dz, body)

    def par_copy(zz):
        return remote(rows(PSEND, zz * HALF, HALF), rows(PRECV, zz * HALF, HALF), par_s.at[zz], par_r.at[zz], peer)

    def process(zz):
        at = pl.ds(pl.multiple_of(zz * HALF, HALF), HALF)

        def half(which):
            columns = pl.ds(pl.multiple_of(which * HALF, HALF), HALF)
            return sum(dot(COT[k, at, :], WRT[k * CW:(k + 1) * CW, columns]) for k in range(NCH))

        PSEND[at, :] = half(1 - t).astype(BF16)
        par_copy(zz).start()
        PART[at, :] = half(t)

    def mine(j):
        return out.at[:, pl.ds(pl.multiple_of(j * HROW + t * HALF, HALF), HALF)]

    def theirs(j):
        return out.at[:, pl.ds(pl.multiple_of(j * HROW + (1 - t) * HALF, HALF), HALF)]

    def out_copy(to):
        return remote(rows(OSEND, to * TOK, TOK), mine(me), out_s.at[to], out_r.at[me], zdev(to))

    def out_in(j):
        return remote(mine(j), mine(j), out_s.at[j], out_r.at[j], zdev(j))

    def orl_copy(j, src=None):
        return remote(mine(j) if src is None else src, mine(j), orl_s.at[j], orl_r.at[j], peer)

    def orl_in(j):
        return remote(theirs(j), theirs(j), orl_s.at[j], orl_r.at[j], peer)

    own_out = pltpu.make_async_copy(rows(OSEND, me * TOK, TOK), mine(me), loc.at[2])

    def out_sum(zz):
        par_copy(zz).wait_recv()
        at = pl.ds(pl.multiple_of(zz * HALF, HALF), HALF)
        OSEND[at, :] = (PART[at, :] + PRECV[at, :].astype(F32)).astype(BF16)

    def out_stage(zz):
        out_sum(zz)
        out_copy(zz * 2).start()
        out_copy(zz * 2 + 1).start()

    def out_relay(dz):
        def body(j):
            out_in(j).wait_recv()
            orl_copy(j).start()
        over(dz, body)

    ones = jnp.ones((BLOCK, BLOCK), BF16)
    scale = factor * 8.0 * BLOCK ** (-0.5)

    def weight(k):
        def piece(n, carry):
            at = pl.multiple_of(n * HALF, HALF)
            acc = dot(AT[pl.ds(at, HALF), :], COT[k]) * scale
            clipped = []
            for b in range(CW // BLOCK):
                x = acc[:, b * BLOCK:(b + 1) * BLOCK]
                mean = dot((x * x).astype(BF16), ones) * (1.0 / BLOCK)
                limit = CLIP * jnp.sqrt(mean + 1e-6)
                clipped.append(jnp.clip(x, -limit, limit).astype(BF16))
            WG[pl.ds(pl.multiple_of(k * HROW + n * HALF, HALF), HALF), :] = jnp.concatenate(clipped, axis=1)
            return carry
        lax.fori_loop(0, HROW // HALF, piece, 0)

    def pick(half, a, b):
        return (1 - half) * a + half * b

    def place(i):
        half = i % 2
        p1, p2 = pick(half, y1, y3) * 2 + xh, pick(half, y3, y1) * 2 + xh
        return p1, p2, pick(half, b1, b2), pick(half, b2, b1), i * 256

    px = {"outer": y * 2 + 1 - xh}

    def ds16(at, n):
        return pl.ds(pl.multiple_of(at, 16), n)

    def rs1_copy(i):
        p1, p2, q1, q2, base = place(i)
        return remote(WG.at[ds16(base + (1 - q1) * 128, 128), :], RS1.at[ds16(i * 128, 128), :],
                      rs_s.at[i], rs_r.at[i], {"outer": p1})

    def rs2_copy(i):
        p1, p2, q1, q2, base = place(i)
        return remote(S2.at[ds16(i * 64, 64), :], RS2.at[ds16(i * 64, 64), :], rs_s.at[8 + i], rs_r.at[8 + i], {"outer": p2})

    def rsx_copy(i):
        return remote(SX.at[ds16(i * 64, 64), :], RSX.at[ds16(i * 64, 64), :], rs_s.at[16 + i], rs_r.at[16 + i], px)

    def combos(body, k):
        body(2 * k)
        body(2 * k + 1)

    def stage2(i):
        p1, p2, q1, q2, base = place(i)
        rs1_copy(i).wait_recv()
        off = (1 - q2) * 64
        S2[ds16(i * 64, 64), :] = (WG[ds16(base + q1 * 128 + off, 64), :].astype(F32)
                                   + RS1[ds16(i * 128 + off, 64), :].astype(F32)).astype(BF16)
        rs2_copy(i).start()

    def stage3(i):
        p1, p2, q1, q2, base = place(i)
        rs2_copy(i).wait_recv()
        SX[ds16(i * 64, 64), :] = (WG[ds16(base + q1 * 128 + q2 * 64, 64), :].astype(F32)
                                   + RS1[ds16(i * 128 + q2 * 64, 64), :].astype(F32)
                                   + RS2[ds16(i * 64, 64), :].astype(F32)).astype(BF16)
        rsx_copy(i).start()

    def ag_row(i, f1, f2):
        p1, p2, q1, q2, base = place(i)
        a = q1 if f1 == 0 else 1 - q1
        b = q2 if f2 == 0 else 1 - q2
        return outw.at[ds16(i % 2 * 256 + a * 128 + b * 64, 64), pl.ds(pl.multiple_of(i // 2 * CW, CW), CW)]

    KIND = ((0, 0), (0, 0), (0, 1))
    FLIP = ((0, 1), (1, 0), (1, 1))

    def ag_copy(i, kind, src=None):
        p1, p2, q1, q2, base = place(i)
        row = ag_row(i, *KIND[kind])
        return remote(row if src is None else src, row, ag_s.at[i * 3 + kind], ag_r.at[i * 3 + kind],
                      {"outer": p2 if kind == 0 else p1})

    def ag_in(i, kind):
        p1, p2, q1, q2, base = place(i)
        row = ag_row(i, *FLIP[kind])
        return remote(row, row, ag_s.at[i * 3 + kind], ag_r.at[i * 3 + kind], {"outer": p2 if kind == 0 else p1})

    def own_fin(i):
        return pltpu.make_async_copy(FIN.at[ds16(i * 64, 64), :], ag_row(i, 0, 0), loc.at[4 + i])

    def stage4(i):
        rsx_copy(i).wait_recv()
        total = SX[ds16(i * 64, 64), :].astype(F32) + RSX[ds16(i * 64, 64), :].astype(F32)
        high = total.astype(BF16)
        low = (total - high.astype(F32)).astype(BF16)
        both = jnp.concatenate([high, low], axis=0)
        pieces = []
        for b in range(CW // BLOCK):
            r = dot(both[:, b * BLOCK:(b + 1) * BLOCK], S)
            pieces.append(((r[:64] + r[64:]) * (BLOCK ** (-0.5))).astype(BF16))
        FIN[ds16(i * 64, 64), :] = jnp.concatenate(pieces, axis=1)
        for kind in range(2):
            ag_copy(i, kind, FIN.at[ds16(i * 64, 64), :]).start()
        own_fin(i).start()

    def stage5(i):
        ag_in(i, 0).wait_recv()
        ag_copy(i, 2).start()

    def stage7(i):
        for kind in (1, 2):
            ag_in(i, kind).wait_recv()

    def send_ring(k, step):
        for half in range(2):
            for direction in range(2):
                if step and goes(direction, step - 1, half):
                    ring_in(direction, k, step - 1, half).wait_recv()
                if step < 4 and goes(direction, step, half):
                    ring(direction, k, step, half).start()
        for dz in ((0,) if step == 0 else (4,) if step == 4 else (-step, step)):
            sib_copy(k, dz, c).start()

    def sib_wait(k, step):
        for dz in ((0,) if step == 0 else (4,) if step == 4 else (-step, step)):
            sib_copy(k, dz, 1 - c).wait_recv()

    SKEW = (0, 0, 3, 3)

    def slot_items(slot):
        return [(k, slot - SKEW[k]) for k in range(NCH) if 0 <= slot - SKEW[k] <= 4]

    SENDS = {0: (4,), 1: (3, 2, 1)}

    def reduce_stage(k):
        for i in (2 * k, 2 * k + 1):
            rs1_copy(i).start()

    def chain(slot, first):
        for k in range(NCH):
            a = slot - first[k]
            if 1 <= a <= 4:
                combos((stage2, stage3, stage4, stage5)[a - 1], k)

    FIRST = (4, 5, 7, 7)
    END = SKEW[-1] + 4
    SUMS = (END - 2, END - 1, END, END)

    for slot in range(END + 1):
        for k, step in slot_items(slot):
            send_ring(k, step)
        for dz in SENDS.get(slot, ()):
            att_send(dz)
        if slot == 0:
            sib_att().start()
            load_w.wait()
            for b in range(DCOL // BLOCK):
                part = slice(b * BLOCK, (b + 1) * BLOCK)
                turned = lax.dot_general(S, WV[:, part], (((0,), (1,)), ((), ())), preferred_element_type=F32)
                WRT[part, :] = (turned * 0.0625).astype(BF16)
            own_act.wait()
            turn(me)
            sib_att_in().wait_recv()
            turn(sib)
        for dz in SENDS.get(slot - 1, ()):
            att_relay(dz)
        for dz in SENDS.get(slot - 2, ()):
            att_finish(dz)
        if slot < END:
            chain(slot, SUMS)
        for k, step in slot_items(slot):
            sib_wait(k, step)
        if slot == END:
            out_stage(zat(2))
            out_stage(zat(-2))
        for k in range(NCH):
            if slot == FIRST[k]:
                weight(k)
                reduce_stage(k)
        if slot == END:
            chain(slot, SUMS)
        if slot == END - 3:
            process(z)
        if slot >= END - 3:
            step = slot - END + 4
            for dz in ((4,) if step == 4 else (-step, step)):
                process(zat(dz))
        if slot == END - 2:
            out_sum(z)
            own_out.start()
            out_copy(sib).start()
            orl_copy(me, rows(OSEND, me * TOK, TOK)).start()
        if slot == END - 1:
            out_stage(zat(1))
            out_stage(zat(-1))
        if slot == END:
            for dz in (3, -3):
                out_stage(zat(dz))
            out_in(sib).wait_recv()
            orl_copy(sib).start()

    out_stage(zat(4))
    out_relay(1)
    chain(END + 1, SUMS)
    out_relay(2)
    for k in range(NCH):
        for direction in range(2):
            for step in range(4):
                for half in range(2):
                    if goes(direction, step, half):
                        ring(direction, k, step, half).wait_send()
        for dz in range(NZ):
            sib_copy(k, dz, c).wait_send()
    sib_att().wait_send()

    def sent(j):
        att_copy(j).wait_send()
        arl_copy(j).wait_send()

    for dz in range(1, 5):
        over(dz, sent)

    def parts(zz, carry):
        par_copy(zz).wait_send()
        return carry

    lax.fori_loop(0, NZ, parts, 0)

    chain(END + 2, SUMS)
    out_relay(3)
    chain(END + 3, SUMS)
    out_relay(4)
    chain(END + 4, SUMS)
    for k in range(NCH):
        combos(stage7, k)

    def all_j(body):
        def step(k, carry):
            body(k)
            return carry
        lax.fori_loop(0, 2 * NZ, step, 0)

    all_j(lambda j: orl_in(j).wait_recv())
    own_out.wait()
    out_copy(sib).wait_send()
    for dz in range(1, 5):
        def body(j):
            out_copy(j).wait_send()
        over(dz, body)
    all_j(lambda j: orl_copy(j).wait_send())

    def sums(i):
        rs1_copy(i).wait_send()
        rs2_copy(i).wait_send()
        rsx_copy(i).wait_send()
        for kind in range(3):
            ag_copy(i, kind).wait_send()
        own_fin(i).wait()

    lax.fori_loop(0, 2 * NCH, lambda i, carry: (sums(i), carry)[1], 0)


def local(attn_out, cotangent, out_weight):
    hbm = pl.BlockSpec(memory_space=pl.ANY)
    dma = pltpu.SemaphoreType.DMA
    tokens = TOK * 2 * NZ
    return pl.pallas_call(
        kernel,
        out_shape=(jax.ShapeDtypeStruct(attn_out.shape, BF16), jax.ShapeDtypeStruct(out_weight.shape, BF16)),
        in_specs=[hbm, hbm, hbm],
        out_specs=(hbm, hbm),
        scratch_shapes=[
            pltpu.VMEM((TOK, DCOL), BF16),
            pltpu.VMEM((NCH, tokens, CW), BF16),
            pltpu.VMEM((HROW, DCOL), BF16),
            pltpu.VMEM((DCOL, HROW), BF16),
            pltpu.VMEM((tokens, HROW), BF16),
            pltpu.VMEM((HROW, tokens), BF16),
            pltpu.VMEM((tokens, HALF), F32),
            pltpu.VMEM((tokens, HALF), BF16),
            pltpu.VMEM((tokens, HALF), BF16),
            pltpu.VMEM((tokens, HALF), BF16),
            pltpu.VMEM((NCH * HROW, CW), BF16),
            pltpu.VMEM((1024, CW), BF16),
            pltpu.VMEM((512, CW), BF16),
            pltpu.VMEM((512, CW), BF16),
            pltpu.VMEM((512, CW), BF16),
            pltpu.VMEM((512, CW), BF16),
            pltpu.VMEM((512, CW), BF16),
            dma((64,)), dma((64,)),
            dma((NCH * NZ,)), dma((NCH * NZ,)),
            dma((16,)), dma((16,)),
            dma((16,)), dma((16,)),
            dma((NZ,)), dma((NZ,)),
            dma((16,)), dma((16,)),
            dma((16,)), dma((16,)),
            dma((24,)), dma((24,)),
            dma((24,)), dma((24,)),
            dma((12,)),
        ],
        compiler_params=pltpu.CompilerParams(
            collective_id=0, has_side_effects=True, vmem_limit_bytes=48 * 1024 * 1024),
    )(attn_out, cotangent, out_weight)


def solution(mesh):
    in_specs = (P(("outer", "dp"), None), P(("outer", "dp"), "tensor"), P("dp", "tensor"))
    out_specs = (P(("outer", "dp"), None), P("dp", "tensor"))
    return jax.shard_map(local, mesh=mesh, in_specs=in_specs, out_specs=out_specs, check_vma=False)
```
